256 devices in a mesh: row: 16 (over y, z_lo, core), col: 16 (over z_hi, x).
Axes of the slice: x: 4, y: 4, z: 8 (z_hi: 4, z_lo: 2; z = z_hi * 2 + z_lo), core: 2. Of those that a mesh axis runs over, the one named last changes fastest.
Arguments:
- final_logits: float32 [64, 131072], P(None, ('row', 'col')), as said below
- labels: int32 [131072], P(('row', 'col')), may hold values from 0 to 63
- features: float32 [64, 131072], P(None, ('row', 'col')), may hold values from -1.25 to 1.25
- tiles: float32 [16, 16, 46, 256, 256], P('row', 'col'), may hold values from -0.078125 to 0.078125
- tile_rows: int32 [16, 16, 46], P('row', 'col'), may hold values from 0 to 31, as said below
- tile_cols: int32 [16, 16, 46], P('row', 'col'), may hold values from 0 to 31, as said below
- live: int32 [16, 16], P('row', 'col'), may hold values from 11 to 46
Outputs:
- grad_start: float32 [64, 131072], P(None, ('row', 'col'))
- teleport_grad: float32 [64, 131072], P(None, ('row', 'col'))
- head_grad: float32 [64, 64], replicated
The draws below stay inside these ranges and needn't reach their ends.
Inputs may be any that keep to these rules, and one draw needn't show every extreme that they name: `final_logits`: entries lie within -400 to 400. `tile_rows`: within one device the slots name distinct (tile row, tile column) pairs. `tile_cols`: within one device the slots name distinct (tile row, tile column) pairs.
All inputs are finite; a program needn't handle non-finite values.
Results may differ from the reference program's by a relative error of at most 0.0003.
Values sent between devices are 32-bit elements; how exact they have to be, the bound alone decides.
A program may use at most 64 MiB of HBM per device.

```python
import jax
import jax.numpy as jnp
from jax import lax

C = 64
F = 64
TILE = 256
NB = 512
TPD = 46
STEPS = 4
NODES = 131072
NTR = 32
NTC = 32
N_ROW = 16
N_COL = 16
DEVICES = 256


def tile_layout(key):
    positions_all = N_COL * NB // TILE * (N_ROW * NB // TILE)
    device_keys = jax.random.split(key, N_ROW * N_COL)

    def one_device(device_key):
        others = jax.random.permutation(device_key, positions_all - 2) + 1
        fixed_ends = jnp.array([0, positions_all - 1], dtype=jnp.int32)
        return jnp.concatenate([fixed_ends, others[:TPD - 2].astype(jnp.int32)])
    positions = jax.vmap(one_device)(device_keys).reshape(N_ROW, N_COL, TPD)
    column_count = N_ROW * NB // TILE
    return (positions // column_count, positions % column_count)


def draw_tile_rows(key, part):
    return tile_layout(key)[0].astype(jnp.int32)


def draw_tile_cols(key, part):
    return tile_layout(key)[1].astype(jnp.int32)


def draw_live(key, part):
    key = jax.random.fold_in(key, 5)
    first_key, second_key = jax.random.split(key)
    lower = max(2, TPD // 4)
    devices_all = N_ROW * N_COL
    counts_drawn = jax.random.randint(first_key, (devices_all,), lower, TPD + 1)
    chosen = jax.random.randint(second_key, (), 0, devices_all)
    places = jnp.arange(devices_all)
    counts_drawn = jnp.where(places == chosen, TPD, counts_drawn)
    counts_drawn = jnp.where(places == (chosen + 1) % devices_all, lower, counts_drawn)
    return counts_drawn.reshape(N_ROW, N_COL).astype(jnp.int32)


def draw_final_logits(key, part):
    key = jax.random.fold_in(key, 11)
    first_key = jax.random.fold_in(key, 0)
    nodes_all = NB * N_ROW * N_COL
    scores = 3.0 * jax.random.normal(first_key, (C, nodes_all))
    return jnp.clip(scores, -400.0, 400.0).astype(jnp.float32)


def place_ends(values, stream_key, smallest, high):
    dims = values.shape
    index_at = [jax.random.randint(jax.random.fold_in(stream_key, axis), (), 0, dims[axis]) for axis in range(len(dims))]
    values = values.at[tuple(index_at)].set(smallest)
    longest = dims.index(max(dims))
    index_at[longest] = (index_at[longest] + 1) % dims[longest]
    return values.at[tuple(index_at)].set(high)


def level_of(own_key, dims, shards, low, top_value):
    factor_of, own = 1.0, jax.random.fold_in(own_key, 6)
    for dim, blocks in shards:
        steps = jnp.exp(jax.random.uniform(jax.random.fold_in(own, dim), (blocks,), jnp.float32, low / len(shards), top_value / len(shards)))
        factor_of = factor_of * jnp.repeat(steps, dims[dim] // blocks).reshape([-1 if axis == dim else 1 for axis in range(len(dims))])
    return factor_of


def bell_draw(key, dims, scale, bound, pieces=(), kind=jnp.bfloat16):
    values = scale * jax.random.normal(key, dims, jnp.float32)
    if pieces:
        values = values * level_of(key, dims, pieces, -0.22, 0.18)
    return jnp.clip(values, -bound, bound).astype(kind)


def setup_inputs(seed: int = 0) -> dict:
    splits = jax.random.split(jax.random.key(seed), 8)
    return {
        "final_logits": draw_final_logits(jax.random.fold_in(splits[7], 71), 0),
        "labels": place_ends(jax.random.randint(splits[1], (NODES,), 0, C), jax.random.fold_in(splits[1], 1), 0, C - 1).astype(jnp.int32),
        "features": bell_draw(splits[2], (F, NODES), (30.0 / (NB * DEVICES) ** 0.5), 1.25, ((1, 256),), jnp.float32),
        "tiles": bell_draw(splits[3], (N_ROW, N_COL, TPD, TILE, TILE), (TILE * TILE * TPD // NB) ** -0.5, 0.078125, ((0, 16), (1, 16)), jnp.float32),
        "tile_rows": draw_tile_rows(jax.random.fold_in(splits[7], 71), 0),
        "tile_cols": draw_tile_cols(jax.random.fold_in(splits[7], 71), 0),
        "live": draw_live(jax.random.fold_in(splits[7], 71), 0),
    }


def propagate(gradient, tiles, tile_rows, tile_cols, live):
    split_field = gradient.reshape(C, N_ROW, N_COL, NB)
    gathered_all = split_field.transpose(2, 0, 1, 3).reshape(N_COL, C, NTC, TILE)

    def per_row(inputs):
        row_tiles, row_rows, row_cols, row_live = inputs
        picked = jax.vmap(lambda blocks, chosen: jnp.take(blocks, chosen, axis=1))(gathered_all, row_cols)
        products = jnp.einsum("ecsj,esji->ecsi", picked, row_tiles, precision=lax.Precision.HIGHEST)
        usable = jnp.arange(TPD, dtype=jnp.int32)[None, :] < row_live[:, None]
        selector = ((row_rows[:, :, None] == jnp.arange(NTR, dtype=jnp.int32)[None, None, :]) & usable[:, :, None]).astype(jnp.float32)
        summed = jnp.einsum("ecsi,esn->cni", products, selector, precision=lax.Precision.HIGHEST)
        return summed.reshape(C, NTR * TILE)

    blocks_out = lax.map(per_row, (tiles, tile_rows, tile_cols, live))
    return blocks_out.transpose(1, 0, 2).reshape(C, NODES)


def reference(final_logits, labels, features, tiles, tile_rows, tile_cols, live):
    probabilities = jax.nn.softmax(final_logits.astype(jnp.float32), axis=0)
    one_hot = (labels[None, :] == jnp.arange(C, dtype=jnp.int32)[:, None]).astype(jnp.float32)
    gradient = probabilities - one_hot
    teleport = jnp.zeros((C, NODES), jnp.float32)
    for step in range(STEPS):
        teleport = teleport + 0.1 * gradient
        gradient = 0.9 * propagate(gradient, tiles, tile_rows, tile_cols, live)
    head_grad = jnp.dot(features, teleport.T, precision=lax.Precision.HIGHEST)
    return gradient, teleport, head_grad
```

```python
import functools

import jax
import jax.numpy as jnp
from jax import lax
from jax.experimental import pallas as pl
from jax.experimental.pallas import tpu as pltpu
from jax.sharding import PartitionSpec as P

MESH = pl.DeviceIdType.MESH
STEPS = 4
CHUNKS = 4
LAG_X = 1
LAG_Z = 2
PIECES = 23

GATHER_ORDER = ((0, 1), (1, 0), (3, 0), (2, 0), (1, 1), (3, 1), (2, 1))


def kernel(
    order,
    logits,
    labels,
    features,
    tiles,
    grad_out,
    tele,
    head_out,
    staged,
    tiles_hi,
    tiles_lo,
    field,
    running,
    gathered,
    outgoing,
    from_x,
    partial,
    from_z,
    head_x,
    head_z,
    head_u,
    head_c,
    tile_sem,
    gs_sem,
    gr_sem,
    fs_sem,
    fr_sem,
    xs_sem,
    xr_sem,
    zs_sem,
    zr_sem,
    hs_sem,
    hr_sem,
):
    slots = tiles.shape[2]
    tile = tiles.shape[3]
    classes, width = logits.shape
    size = classes // CHUNKS
    halves = width // tile
    total = STEPS * CHUNKS
    row = lax.axis_index("row")
    col = lax.axis_index("col")
    core = lax.rem(row, 2)
    unit = row // 2
    y = unit // 2
    z_lo = lax.rem(unit, 2)
    x = lax.rem(col, 4)
    z_hi = col // 4

    def place(dy, dz):
        return lax.rem(y + dy, 4) * 2 + lax.rem(z_lo + dz, 2)

    def at_unit(dy, dz):
        return {"row": place(dy, dz) * 2 + core, "col": col}

    def at_x(dx):
        return {"row": row, "col": z_hi * 4 + lax.rem(x + dx, 4)}

    def at_z(dz):
        return {"row": row, "col": lax.rem(z_hi + dz, 4) * 4 + x}

    partner = {"row": unit * 2 + 1 - core, "col": col}

    def remote(src, dst, send, recv, device):
        return pltpu.make_async_remote_copy(
            src_ref=src,
            dst_ref=dst,
            send_sem=send,
            recv_sem=recv,
            device_id=device,
            device_id_type=MESH,
        )

    per_piece = slots // PIECES

    def load_piece(i):
        part = pl.ds(i * per_piece, per_piece)
        return pltpu.make_async_copy(tiles.at[0, 0, part], staged.at[part], tile_sem.at[i])

    def start_piece(i, carry):
        load_piece(i).start()
        return carry

    lax.fori_loop(0, PIECES, start_piece, 0)

    barrier = pltpu.get_barrier_semaphore()
    peers = [at_unit(dy, dz) for dy, dz in GATHER_ORDER]
    peers += [at_x(d) for d in (1, 2, 3)] + [at_z(d) for d in (1, 2, 3)] + [partner]
    for device in peers:
        pl.semaphore_signal(barrier, inc=1, device_id=device, device_id_type=MESH)

    scores = logits[...]
    powers = jnp.exp(scores - jnp.max(scores, axis=0, keepdims=True))
    probabilities = powers / jnp.sum(powers, axis=0, keepdims=True)
    class_index = lax.broadcasted_iota(jnp.int32, (classes, width), 0)
    first = probabilities - (class_index == labels[...]).astype(jnp.float32)
    tele[...] = 0.1 * first
    mine = core * 8 + unit
    for q in range(CHUNKS):
        gathered[0, q, mine] = first[q * size : (q + 1) * size]
    pl.semaphore_wait(barrier, len(peers))

    def gather_copy(par, q, i):
        dy, dz = GATHER_ORDER[i]
        block = gathered.at[par, q, mine]
        return remote(block, block, gs_sem.at[q, i], gr_sem.at[par, q, i], at_unit(dy, dz))

    def hand_copy(par, q, i):
        dy, dz = (((0, 0),) + GATHER_ORDER)[i]
        slot = place(4 - dy, dz)
        block = gathered.at[par, q, core * 8 + slot]
        return remote(block, block, fs_sem.at[q, i], fr_sem.at[par, q, i], partner)

    def x_copy(par, q, d):
        return remote(
            outgoing.at[q, lax.rem(x + d, 4)],
            from_x.at[par, q, d - 1],
            xs_sem.at[q, d - 1],
            xr_sem.at[par, q, d - 1],
            at_x(d),
        )

    def z_copy(par, q, d):
        return remote(
            partial.at[q, lax.rem(z_hi + d, 4)],
            from_z.at[par, q, d - 1],
            zs_sem.at[q, d - 1],
            zr_sem.at[par, q, d - 1],
            at_z(d),
        )

    def split(i):
        step, q = i // CHUNKS, lax.rem(i, CHUNKS)
        return step, q, lax.rem(step, 2)

    def send_gather(par, q):
        for i in reversed(range(len(GATHER_ORDER))):
            gather_copy(par, q, i).start()
        hand_copy(par, q, 0).start()

    def hand_over(i):
        _, q, par = split(i)
        for n in range(len(GATHER_ORDER)):
            gather_copy(par, q, n).wait_recv()
            hand_copy(par, q, n + 1).start()
        for n in range(len(GATHER_ORDER)):
            gather_copy(par, q, n).wait_send()

    def multiply(i):
        _, q, par = split(i)
        for n in range(len(GATHER_ORDER) + 1):
            hand_copy(par, q, n).wait()
        for c in range(2):
            for u in range(8):
                for h in range(halves):
                    value = gathered[par, q, c * 8 + u, :, h * tile : (h + 1) * tile]
                    high = value.astype(jnp.bfloat16)
                    low = (value - high.astype(jnp.float32)).astype(jnp.bfloat16)
                    field[(u * 2 + c) * halves + h] = jnp.concatenate([high, low], axis=0)
        carried = jnp.zeros((size, tile), jnp.float32)
        for s in range(slots):
            slot = order[0, s]
            both = field[order[1, s]]
            by_high = jnp.dot(both, tiles_hi[slot], preferred_element_type=jnp.float32)
            by_low = jnp.dot(both[:size], tiles_lo[slot], preferred_element_type=jnp.float32)
            product = by_high[:size] + by_high[size:] + by_low
            carried = product + order[2, s].astype(jnp.float32) * carried
            running[s] = carried
        for n in range(32):
            block, h = n // halves, n % halves
            outgoing[q, block % 4, block // 4, :, h * tile : (h + 1) * tile] = running[order[3, n]]
        for d in (2, 1, 3):
            x_copy(par, q, d).start()

    def reduce_x(i):
        _, q, par = split(i)
        for d in (1, 3, 2):
            x_copy(par, q, d).wait()
        for b in range(4):
            partial[q, b] = (
                outgoing[q, x, b] + from_x[par, q, 0, b] + from_x[par, q, 2, b]
            ) + from_x[par, q, 1, b]
        for d in (2, 1, 3):
            z_copy(par, q, d).start()

    def reduce_z(i):
        step, q, par = split(i)
        for d in (1, 3, 2):
            z_copy(par, q, d).wait()
        value = 0.9 * (
            (partial[q, z_hi] + from_z[par, q, 0] + from_z[par, q, 2]) + from_z[par, q, 1]
        )
        rows = pl.ds(pl.multiple_of(q * size, size), size)

        @pl.when(step < STEPS - 1)
        def _():
            gathered[1 - par, q, mine] = value
            send_gather(1 - par, q)
            tele[rows] = tele[rows] + 0.1 * value

        @pl.when(step == STEPS - 1)
        def _():
            grad_out[rows] = value

    def head_copies(stage):
        if stage == 0:
            return [
                remote(head_x.at[x], head_x.at[x], hs_sem.at[d - 1], hr_sem.at[d - 1], at_x(d))
                for d in (2, 1, 3)
            ]
        if stage == 1:
            return [
                remote(
                    head_z.at[z_hi], head_z.at[z_hi], hs_sem.at[d + 2], hr_sem.at[d + 2], at_z(d)
                )
                for d in (2, 1, 3)
            ]
        if stage == 2:
            return [
                remote(
                    head_u.at[unit],
                    head_u.at[unit],
                    hs_sem.at[6 + i],
                    hr_sem.at[6 + i],
                    at_unit(*GATHER_ORDER[i]),
                )
                for i in range(len(GATHER_ORDER))
            ]
        return [remote(head_c.at[core], head_c.at[core], hs_sem.at[13], hr_sem.at[13], partner)]

    def head_stage(stage):
        if stage == 0:
            value = lax.dot_general(
                features[...],
                tele[...],
                (((1,), (1,)), ((), ())),
                precision=lax.Precision.HIGHEST,
                preferred_element_type=jnp.float32,
            )
        else:
            for copy in head_copies(stage - 1):
                copy.wait()
            source = (head_x, head_z, head_u, head_c)[stage - 1]
            value = source[0]
            for n in range(1, source.shape[0]):
                value = value + source[n]
        if stage == 0:
            head_x[x] = value
        elif stage == 1:
            head_z[z_hi] = value
        elif stage == 2:
            head_u[unit] = value
        elif stage == 3:
            head_c[core] = value
        else:
            head_out[...] = value
        if stage < 4:
            for copy in head_copies(stage):
                copy.start()

    for q in range(CHUNKS):
        send_gather(0, q)

    def convert_piece(i, carry):
        load_piece(i).wait()
        for n in range(per_piece):
            value = staged[i * per_piece + n]
            high = value.astype(jnp.bfloat16)
            tiles_hi[i * per_piece + n] = high
            tiles_lo[i * per_piece + n] = (value - high.astype(jnp.float32)).astype(jnp.bfloat16)
        return carry

    lax.fori_loop(0, PIECES, convert_piece, 0)
    running[slots] = jnp.zeros((size, tile), jnp.float32)
    hand_over(0)

    head_from = (STEPS - 1) * CHUNKS - 1 + LAG_Z

    def turn(j, carry):
        @pl.when(j < total)
        def _():
            multiply(j)

        @pl.when((j >= LAG_X) & (j < total + LAG_X))
        def _():
            reduce_x(j - LAG_X)

        @pl.when(j >= LAG_Z)
        def _():
            reduce_z(j - LAG_Z)

        @pl.when(j + 1 < total)
        def _():
            hand_over(j + 1)

        for stage in range(5):

            @pl.when(j == head_from + stage)
            def _():
                head_stage(stage)

        return carry

    lax.fori_loop(0, total + LAG_Z, turn, 0)


def slot_order(tile_rows, tile_cols, live, row_count):
    slots = tile_rows.shape[0]
    index = jnp.arange(slots, dtype=jnp.int32)
    key = jnp.where(index < live, tile_rows, row_count)
    before = (key[None, :] < key[:, None]) | (
        (key[None, :] == key[:, None]) & (index[None, :] < index[:, None])
    )
    rank = jnp.sum(before.astype(jnp.int32), axis=1)
    chosen = rank[None, :] == index[:, None]
    slot = jnp.sum(jnp.where(chosen, index[None, :], 0), axis=1)
    column = jnp.sum(jnp.where(chosen, tile_cols[None, :], 0), axis=1)
    row = jnp.sum(jnp.where(chosen, key[None, :], 0), axis=1)
    keep = jnp.concatenate([jnp.zeros((1,), jnp.int32), (row[1:] == row[:-1]).astype(jnp.int32)])
    rows = jnp.arange(row_count, dtype=jnp.int32)
    upto = jnp.sum((key[None, :] <= rows[:, None]).astype(jnp.int32), axis=1)
    some = jnp.any(key[None, :] == rows[:, None], axis=1)
    last = jnp.where(some, upto - 1, slots)
    last = jnp.concatenate([last, jnp.full((slots - row_count,), slots, jnp.int32)])
    return jnp.stack([slot, column, keep, last])


def shards(final_logits, labels, features, tiles, tile_rows, tile_cols, live):
    classes, width = final_logits.shape
    units = features.shape[0]
    slots, tile = tiles.shape[2], tiles.shape[3]
    size = classes // CHUNKS
    row_count = 16 * width // tile
    order = slot_order(tile_rows[0, 0], tile_cols[0, 0], live[0, 0], row_count)
    f32 = jnp.float32
    vmem = pl.BlockSpec(memory_space=pltpu.VMEM)
    dma = pltpu.SemaphoreType.DMA
    return pl.pallas_call(
        kernel,
        out_shape=(
            jax.ShapeDtypeStruct((classes, width), f32),
            jax.ShapeDtypeStruct((classes, width), f32),
            jax.ShapeDtypeStruct((units, classes), f32),
        ),
        in_specs=[
            pl.BlockSpec(memory_space=pltpu.SMEM),
            vmem,
            vmem,
            vmem,
            pl.BlockSpec(memory_space=pl.ANY),
        ],
        out_specs=(vmem, vmem, vmem),
        scratch_shapes=[
            pltpu.VMEM((slots, tile, tile), f32),
            pltpu.VMEM((slots, tile, tile), jnp.bfloat16),
            pltpu.VMEM((slots, tile, tile), jnp.bfloat16),
            pltpu.VMEM((row_count, 2 * size, tile), jnp.bfloat16),
            pltpu.VMEM((slots + 1, size, tile), f32),
            pltpu.VMEM((2, CHUNKS, 16, size, width), f32),
            pltpu.VMEM((CHUNKS, 4, 4, size, width), f32),
            pltpu.VMEM((2, CHUNKS, 3, 4, size, width), f32),
            pltpu.VMEM((CHUNKS, 4, size, width), f32),
            pltpu.VMEM((2, CHUNKS, 3, size, width), f32),
            pltpu.VMEM((4, units, classes), f32),
            pltpu.VMEM((4, units, classes), f32),
            pltpu.VMEM((8, units, classes), f32),
            pltpu.VMEM((2, units, classes), f32),
            dma((PIECES,)),
            dma((CHUNKS, 7)),
            dma((2, CHUNKS, 7)),
            dma((CHUNKS, 8)),
            dma((2, CHUNKS, 8)),
            dma((CHUNKS, 3)),
            dma((2, CHUNKS, 3)),
            dma((CHUNKS, 3)),
            dma((2, CHUNKS, 3)),
            dma((14,)),
            dma((14,)),
        ],
        compiler_params=pltpu.CompilerParams(
            collective_id=0, has_side_effects=True, vmem_limit_bytes=56 * 2**20
        ),
        cost_estimate=pl.CostEstimate(
            flops=3 * 2 * STEPS * slots * classes * tile * tile,
            bytes_accessed=slots * tile * tile * 4,
            transcendentals=classes * width,
        ),
    )(order, final_logits, labels.reshape(1, width), features, tiles)


def solution(mesh):
    in_specs = (
        P(None, ("row", "col")),
        P(("row", "col")),
        P(None, ("row", "col")),
        P("row", "col", None, None, None),
        P("row", "col", None),
        P("row", "col", None),
        P("row", "col"),
    )
    out_specs = (P(None, ("row", "col")), P(None, ("row", "col")), P())
    return jax.shard_map(shards, mesh=mesh, in_specs=in_specs, out_specs=out_specs, check_vma=False)
```

```python
import functools

import jax
import jax.numpy as jnp
from jax import lax
from jax.experimental import pallas as pl
from jax.experimental.pallas import tpu as pltpu
from jax.sharding import PartitionSpec as P

MESH = pl.DeviceIdType.MESH
STEPS = 4
CHUNKS = 4
LAG_X = 1
LAG_Z = 2
PIECES = 23
DISTANCES = (2, 1, 3, 0)
PARTS = ((0, 1), (1, 2), (3, 1))

GATHER_ORDER = ((0, 1), (1, 0), (1, 1), (3, 0), (3, 1), (2, 0), (2, 1))
HAND_AFTER = {0: 0, 2: 1, 4: 3, 6: 2}


def kernel(
    live,
    tile_rows,
    tile_cols,
    labels,
    logits_far,
    features_far,
    tiles,
    grad_out,
    tele,
    head_out,
    logits,
    features,
    order_rows,
    order,
    staged,
    tiles_hi,
    tiles_lo,
    field,
    running,
    gathered,
    outgoing,
    from_x,
    partial,
    from_z,
    head_x,
    head_z,
    head_u,
    head_c,
    tile_sem,
    gs_sem,
    gr_sem,
    fs_sem,
    fr_sem,
    xs_sem,
    xr_sem,
    zs_sem,
    zr_sem,
    hs_sem,
    hr_sem,
    near_sem,
):
    slots = tiles.shape[2]
    tile = tiles.shape[3]
    classes, width = logits.shape
    size = classes // CHUNKS
    halves = width // tile
    total = STEPS * CHUNKS
    row_tiles = 16 * halves
    row = lax.axis_index("row")
    col = lax.axis_index("col")
    core = lax.rem(row, 2)
    unit = row // 2
    y = unit // 2
    z_lo = lax.rem(unit, 2)
    x = lax.rem(col, 4)
    z_hi = col // 4

    def place(dy, dz):
        return lax.rem(y + dy, 4) * 2 + lax.rem(z_lo + dz, 2)

    def at_unit(dy, dz):
        return {"row": place(dy, dz) * 2 + core, "col": col}

    def at_x(dx):
        return {"row": row, "col": z_hi * 4 + lax.rem(x + dx, 4)}

    def at_z(dz):
        return {"row": row, "col": lax.rem(z_hi + dz, 4) * 4 + x}

    partner = {"row": unit * 2 + 1 - core, "col": col}

    def remote(src, dst, send, recv, device):
        return pltpu.make_async_remote_copy(
            src_ref=src,
            dst_ref=dst,
            send_sem=send,
            recv_sem=recv,
            device_id=device,
            device_id_type=MESH,
        )

    per_piece = slots // PIECES

    def load_piece(i):
        part = pl.ds(i * per_piece, per_piece)
        return pltpu.make_async_copy(tiles.at[0, 0, part], staged.at[part], tile_sem.at[i])

    def start_piece(i, carry):
        load_piece(i).start()
        return carry

    load_logits = pltpu.make_async_copy(logits_far, logits, near_sem.at[0])
    load_features = pltpu.make_async_copy(features_far, features, near_sem.at[1])
    load_logits.start()

    barrier = pltpu.get_barrier_semaphore()
    peers = [at_unit(dy, dz) for dy, dz in GATHER_ORDER]
    peers += [at_x(d) for d in (1, 2, 3)] + [at_z(d) for d in (1, 2, 3)] + [partner]
    for device in peers:
        pl.semaphore_signal(barrier, inc=1, device_id=device, device_id_type=MESH)

    lax.fori_loop(0, PIECES, start_piece, 0)
    load_features.start()
    load_logits.wait()
    scores = logits[...]
    powers = jnp.exp(scores - jnp.max(scores, axis=0, keepdims=True))
    probabilities = powers / jnp.sum(powers, axis=0, keepdims=True)
    class_index = lax.broadcasted_iota(jnp.int32, (classes, width), 0)
    first = probabilities - (class_index == labels[...]).astype(jnp.float32)
    tele[...] = 0.1 * first
    mine = core * 8 + unit
    for q in range(CHUNKS):
        gathered[0, q, mine] = first[q * size : (q + 1) * size]
    listed = slot_order(tile_rows[...], tile_cols[...], live[0, 0], row_tiles)
    for n in range(4):
        order_rows[n : n + 1, : listed[n].shape[1]] = listed[n]
    load_order = pltpu.make_async_copy(order_rows, order, near_sem.at[2])
    load_order.start()
    pl.semaphore_wait(barrier, len(peers))

    def gather_copy(par, q, i):
        dy, dz = GATHER_ORDER[i]
        block = gathered.at[par, q, mine]
        return remote(block, block, gs_sem.at[q, i], gr_sem.at[par, q, i], at_unit(dy, dz))

    def hand_copy(par, q, i):
        slot = lax.rem(y + 4 - i, 4) * 2
        block = gathered.at[par, q, pl.ds(core * 8 + slot, 2)]
        return remote(block, block, fs_sem.at[q, i], fr_sem.at[par, q, i], partner)

    def z_place(block):
        distance = lax.rem(block - z_hi + 4, 4)
        own, two, three = (4 - distance) // 4, (distance // 2) * (3 - distance), distance // 3
        return 1 + 2 * own - two + three

    def x_copy(par, q, d, p):
        blocks = pl.ds(*PARTS[p])
        return remote(
            outgoing.at[q, lax.rem(x + d, 4), blocks],
            from_x.at[par, q, d - 1, blocks],
            xs_sem.at[q, d - 1, p],
            xr_sem.at[par, q, d - 1, p],
            at_x(d),
        )

    def z_copy(par, q, d):
        return remote(
            partial.at[q, DISTANCES.index(d)],
            from_z.at[par, q, d - 1],
            zs_sem.at[q, d - 1],
            zr_sem.at[par, q, d - 1],
            at_z(d),
        )

    def split(i):
        step, q = i // CHUNKS, lax.rem(i, CHUNKS)
        return step, q, lax.rem(step, 2)

    def send_gather(par, q):
        for i in reversed(range(len(GATHER_ORDER))):
            gather_copy(par, q, i).start()

    def fill_field(par, q, c):
        for u in range(8):
            for h in range(halves):
                value = gathered[par, q, c * 8 + u, :, h * tile : (h + 1) * tile]
                high = value.astype(jnp.bfloat16).astype(jnp.float32)
                both = jnp.concatenate([high, value - high], axis=0)
                field[(u * 2 + c) * halves + h] = both.astype(jnp.bfloat16)

    def hand_over(i):
        _, q, par = split(i)
        for n in range(len(GATHER_ORDER)):
            gather_copy(par, q, n).wait_recv()
            if n in HAND_AFTER:
                hand_copy(par, q, HAND_AFTER[n]).start()
        fill_field(par, q, core)
        for n in range(len(GATHER_ORDER)):
            gather_copy(par, q, n).wait_send()

    def multiply(i):
        _, q, par = split(i)
        for n in range(4):
            hand_copy(par, q, n).wait()
        fill_field(par, q, 1 - core)
        carried = jnp.zeros((size, tile), jnp.float32)
        for s in range(slots):
            slot = order[0, s]
            both = field[order[1, s]]
            by_high = jnp.dot(both, tiles_hi[slot], preferred_element_type=jnp.float32)
            if size % 16 == 0:
                both = both[:size]
            by_low = jnp.dot(both, tiles_lo[slot], preferred_element_type=jnp.float32)
            product = by_high[:size] + by_high[size:] + by_low[:size]
            if size % 16:
                product = product + by_low[size:]
            carried = product + order[2, s].astype(jnp.float32) * carried
            running[s] = carried
        for n in range(row_tiles):
            block, h = n // halves, n % halves
            outgoing[q, block % 4, z_place(block // 4), :, h * tile : (h + 1) * tile] = running[order[3, n]]
        for p in range(len(PARTS)):
            for d in (2, 1, 3):
                x_copy(par, q, d, p).start()

    def reduce_x(i, p):
        _, q, par = split(i)
        for d in (1, 3, 2):
            x_copy(par, q, d, p).wait()
        start, count = PARTS[p]
        for b in range(start, start + count):
            partial[q, b] = (
                outgoing[q, x, b] + from_x[par, q, 0, b] + from_x[par, q, 2, b]
            ) + from_x[par, q, 1, b]
        for d in (2, 1, 3):
            if d in DISTANCES[start : start + count]:
                z_copy(par, q, d).start()

    def reduce_z(i):
        step, q, par = split(i)
        reduce_x(i, len(PARTS) - 1)
        for d in (1, 3, 2):
            z_copy(par, q, d).wait()
        value = 0.9 * ((partial[q, 3] + from_z[par, q, 0] + from_z[par, q, 2]) + from_z[par, q, 1])
        rows = pl.ds(pl.multiple_of(q * size, size), size)

        @pl.when(step < STEPS - 1)
        def _():
            gathered[1 - par, q, mine] = value
            send_gather(1 - par, q)
            tele[rows] = tele[rows] + 0.1 * value

        @pl.when(step == STEPS - 1)
        def _():
            grad_out[rows] = value

    def head_copies(stage):
        if stage == 0:
            return [
                remote(head_x.at[x], head_x.at[x], hs_sem.at[d - 1], hr_sem.at[d - 1], at_x(d))
                for d in (2, 1, 3)
            ]
        if stage == 1:
            return [
                remote(
                    head_z.at[z_hi], head_z.at[z_hi], hs_sem.at[d + 2], hr_sem.at[d + 2], at_z(d)
                )
                for d in (2, 1, 3)
            ]
        if stage == 2:
            return [
                remote(
                    head_u.at[unit],
                    head_u.at[unit],
                    hs_sem.at[6 + i],
                    hr_sem.at[6 + i],
                    at_unit(*GATHER_ORDER[i]),
                )
                for i in range(len(GATHER_ORDER))
            ]
        return [remote(head_c.at[core], head_c.at[core], hs_sem.at[13], hr_sem.at[13], partner)]

    def head_stage(stage):
        if stage == 0:
            value = lax.dot_general(
                features[...],
                tele[...],
                (((1,), (1,)), ((), ())),
                precision=lax.Precision.HIGHEST,
                preferred_element_type=jnp.float32,
            )
        else:
            for copy in head_copies(stage - 1):
                copy.wait()
            source = (head_x, head_z, head_u, head_c)[stage - 1]
            value = source[0]
            for n in range(1, source.shape[0]):
                value = value + source[n]
        if stage == 0:
            head_x[x] = value
        elif stage == 1:
            head_z[z_hi] = value
        elif stage == 2:
            head_u[unit] = value
        elif stage == 3:
            head_c[core] = value
        else:
            head_out[...] = value
        if stage < 4:
            for copy in head_copies(stage):
                copy.start()

    send_gather(0, 0)

    def convert_piece(i, carry):
        load_piece(i).wait()
        for n in range(per_piece):
            value = staged[i * per_piece + n]
            high = value.astype(jnp.bfloat16)
            tiles_hi[i * per_piece + n] = high
            tiles_lo[i * per_piece + n] = (value - high.astype(jnp.float32)).astype(jnp.bfloat16)
        return carry

    lax.fori_loop(0, PIECES, convert_piece, 0)
    load_order.wait()
    load_features.wait()
    running[slots] = jnp.zeros((size, tile), jnp.float32)
    hand_over(0)
    for q in range(1, CHUNKS):
        send_gather(0, q)

    head_from = (STEPS - 1) * CHUNKS - 1 + LAG_Z

    def turn(j, carry):
        @pl.when(j < total)
        def _():
            multiply(j)

        @pl.when((j >= LAG_X) & (j < total + LAG_X))
        def _():
            reduce_x(j - LAG_X, 0)
            reduce_x(j - LAG_X, 1)

        @pl.when(j >= LAG_Z)
        def _():
            reduce_z(j - LAG_Z)

        @pl.when(j + 1 < total)
        def _():
            hand_over(j + 1)

        for stage in range(5):

            @pl.when(j == head_from + stage)
            def _():
                head_stage(stage)

        return carry

    lax.fori_loop(0, total + LAG_Z, turn, 0)


def hand_out(*refs):
    for source, target in zip(refs[:3], refs[3:]):
        target[...] = source[...]


def slot_order(tile_rows, tile_cols, live, row_count):
    slots = tile_rows.shape[1]

    def index(shape, dim):
        return lax.broadcasted_iota(jnp.int32, shape, dim)

    def total(values, dim):
        return jnp.sum(values, axis=dim, keepdims=True)

    def upright(values):
        square = (slots, slots)
        return total(jnp.where(index(square, 0) == index(square, 1), values, 0), 1)

    across = index((1, slots), 1)
    down = index((slots, 1), 0)
    key = jnp.where(across < live, tile_rows, row_count) * slots + across
    key_down = upright(key)
    rank = total(jnp.where(key < key_down, 1, 0), 1)
    chosen = rank == across
    slot = total(jnp.where(chosen, down, 0), 0)
    column = total(jnp.where(chosen, upright(tile_cols), 0), 0)
    place = index((1, 128), 1)
    starts = place * slots
    upto = total(jnp.where(key_down < starts + slots, 1, 0), 0)
    below = total(jnp.where(key_down < starts, 1, 0), 0)
    last = jnp.where(upto > below, upto - 1, slots)
    first = total(jnp.where(chosen, total(jnp.where(key < key_down - upright(across), 1, 0), 1), 0), 0)
    keep = jnp.where(first < across, 1, 0)
    return slot, column, keep, last


def shards(final_logits, labels, features, tiles, tile_rows, tile_cols, live):
    classes, width = final_logits.shape
    units = features.shape[0]
    slots, tile = tiles.shape[2], tiles.shape[3]
    size = classes // CHUNKS
    row_count = 16 * width // tile
    f32 = jnp.float32
    vmem = pl.BlockSpec(memory_space=pltpu.VMEM)
    far = pl.BlockSpec(memory_space=pl.ANY)
    dma = pltpu.SemaphoreType.DMA
    parts = pl.pallas_call(
        kernel,
        out_shape=(
            jax.ShapeDtypeStruct((classes, width), f32),
            jax.ShapeDtypeStruct((classes, width), f32),
            jax.ShapeDtypeStruct((units, classes), f32),
        ),
        in_specs=[
            pl.BlockSpec(memory_space=pltpu.SMEM),
            vmem,
            vmem,
            vmem,
            far,
            far,
            far,
        ],
        out_specs=(vmem, vmem, vmem),
        scratch_shapes=[
            pltpu.VMEM((classes, width), f32),
            pltpu.VMEM((units, width), f32),
            pltpu.VMEM((4, 128), jnp.int32),
            pltpu.SMEM((4, 128), jnp.int32),
            pltpu.VMEM((slots, tile, tile), f32),
            pltpu.VMEM((slots, tile, tile), jnp.bfloat16),
            pltpu.VMEM((slots, tile, tile), jnp.bfloat16),
            pltpu.VMEM((row_count, 2 * size, tile), jnp.bfloat16),
            pltpu.VMEM((slots + 1, size, tile), f32),
            pltpu.VMEM((2, CHUNKS, 16, size, width), f32),
            pltpu.VMEM((CHUNKS, 4, 4, size, width), f32),
            pltpu.VMEM((2, CHUNKS, 3, 4, size, width), f32),
            pltpu.VMEM((CHUNKS, 4, size, width), f32),
            pltpu.VMEM((2, CHUNKS, 3, size, width), f32),
            pltpu.VMEM((4, units, classes), f32),
            pltpu.VMEM((4, units, classes), f32),
            pltpu.VMEM((8, units, classes), f32),
            pltpu.VMEM((2, units, classes), f32),
            dma((PIECES,)),
            dma((CHUNKS, 7)),
            dma((2, CHUNKS, 7)),
            dma((CHUNKS, 4)),
            dma((2, CHUNKS, 4)),
            dma((CHUNKS, 3, len(PARTS))),
            dma((2, CHUNKS, 3, len(PARTS))),
            dma((CHUNKS, 3)),
            dma((2, CHUNKS, 3)),
            dma((14,)),
            dma((14,)),
            dma((3,)),
        ],
        compiler_params=pltpu.CompilerParams(
            collective_id=0, has_side_effects=True, vmem_limit_bytes=56 * 2**20
        ),
        cost_estimate=pl.CostEstimate(
            flops=3 * 2 * STEPS * slots * classes * tile * tile,
            bytes_accessed=slots * tile * tile * 4,
            transcendentals=classes * width,
        ),
    )(
        live,
        tile_rows[0],
        tile_cols[0],
        labels.reshape(1, width),
        final_logits,
        features,
        tiles,
    )
    return pl.pallas_call(
        hand_out,
        out_shape=tuple(jax.ShapeDtypeStruct(part.shape, f32) for part in parts),
        in_specs=[vmem] * 3,
        out_specs=(vmem,) * 3,
    )(*parts)


def solution(mesh):
    in_specs = (
        P(None, ("row", "col")),
        P(("row", "col")),
        P(None, ("row", "col")),
        P("row", "col", None, None, None),
        P("row", "col", None),
        P("row", "col", None),
        P("row", "col"),
    )
    out_specs = (P(None, ("row", "col")), P(None, ("row", "col")), P())
    return jax.shard_map(shards, mesh=mesh, in_specs=in_specs, out_specs=out_specs, check_vma=False)
```

```python
import functools

import jax
import jax.numpy as jnp
from jax import lax
from jax.experimental import pallas as pl
from jax.experimental.pallas import tpu as pltpu
from jax.sharding import PartitionSpec as P

MESH = pl.DeviceIdType.MESH
STEPS = 4
CHUNKS = 4
LAG_X = 1
LAG_Z = 2
PIECES = 23
DISTANCES = (2, 1, 3, 0)
PARTS = ((0, 1), (1, 2), (3, 1))

GATHER_ORDER = ((0, 1), (1, 0), (1, 1), (3, 0), (3, 1), (2, 0), (2, 1))


def kernel(
    live,
    tile_rows,
    tile_cols,
    labels,
    logits_far,
    features_far,
    tiles,
    grad_out,
    tele,
    head_out,
    logits,
    features,
    order_rows,
    order,
    staged,
    tiles_hi,
    tiles_lo,
    field,
    running,
    gathered,
    outgoing,
    from_x,
    partial,
    from_z,
    head_x,
    head_z,
    head_u,
    head_c,
    tile_sem,
    gs_sem,
    gr_sem,
    fs_sem,
    fr_sem,
    xs_sem,
    xr_sem,
    zs_sem,
    zr_sem,
    hs_sem,
    hr_sem,
    near_sem,
):
    slots = tiles.shape[2]
    tile = tiles.shape[3]
    classes, width = logits.shape
    size = classes // CHUNKS
    halves = width // tile
    total = STEPS * CHUNKS
    row_tiles = 16 * halves
    row = lax.axis_index("row")
    col = lax.axis_index("col")
    core = lax.rem(row, 2)
    unit = row // 2
    y = unit // 2
    z_lo = lax.rem(unit, 2)
    x = lax.rem(col, 4)
    z_hi = col // 4

    def place(dy, dz):
        return lax.rem(y + dy, 4) * 2 + lax.rem(z_lo + dz, 2)

    def at_unit(dy, dz):
        return {"row": place(dy, dz) * 2 + core, "col": col}

    def at_x(dx):
        return {"row": row, "col": z_hi * 4 + lax.rem(x + dx, 4)}

    def at_z(dz):
        return {"row": row, "col": lax.rem(z_hi + dz, 4) * 4 + x}

    def z_place(block):
        distance = lax.rem(block - z_hi + 4, 4)
        own, two, three = (4 - distance) // 4, (distance // 2) * (3 - distance), distance // 3
        return 1 + 2 * own - two + three

    partner = {"row": unit * 2 + 1 - core, "col": col}

    def remote(src, dst, send, recv, device):
        return pltpu.make_async_remote_copy(
            src_ref=src,
            dst_ref=dst,
            send_sem=send,
            recv_sem=recv,
            device_id=device,
            device_id_type=MESH,
        )

    def wait_bytes(ref, sem):
        pltpu.make_async_copy(ref, ref, sem).wait()

    per_piece = slots // PIECES

    def load_piece(i):
        part = pl.ds(i * per_piece, per_piece)
        return pltpu.make_async_copy(tiles.at[0, 0, part], staged.at[part], tile_sem.at[i])

    def start_piece(i, carry):
        load_piece(i).start()
        return carry

    load_logits = pltpu.make_async_copy(logits_far, logits, near_sem.at[0])
    load_features = pltpu.make_async_copy(features_far, features, near_sem.at[1])
    load_logits.start()

    barrier = pltpu.get_barrier_semaphore()
    unit_peers = [at_unit(dy, dz) for dy, dz in GATHER_ORDER]
    x_peers = [at_x(d) for d in range(4)]
    z_peers = [at_z(d) for d in range(4)]
    x_slots = [lax.rem(x + d, 4) for d in range(4)]
    z_slots = [z_place(block) for block in range(4)]
    y_units = [lax.rem(y + 4 - d, 4) * 2 for d in range(4)]
    hand_slots = [core * 8 + u for u in y_units]
    peers = unit_peers + x_peers[1:] + z_peers[1:] + [partner]
    for device in peers:
        pl.semaphore_signal(barrier, inc=1, device_id=device, device_id_type=MESH)

    lax.fori_loop(0, PIECES, start_piece, 0)
    load_features.start()
    load_logits.wait()
    scores = logits[...]
    powers = jnp.exp(scores - jnp.max(scores, axis=0, keepdims=True))
    probabilities = powers / jnp.sum(powers, axis=0, keepdims=True)
    class_index = lax.broadcasted_iota(jnp.int32, (classes, width), 0)
    first = probabilities - (class_index == labels[...]).astype(jnp.float32)
    tele[...] = 0.1 * first
    mine = core * 8 + unit
    for q in range(CHUNKS):
        gathered[0, q, mine] = first[q * size : (q + 1) * size]
    listed = slot_order(tile_rows[...], tile_cols[...], live[0, 0], row_tiles)
    for n in range(4):
        order_rows[n : n + 1, : listed[n].shape[1]] = listed[n]
    load_order = pltpu.make_async_copy(order_rows, order, near_sem.at[2])
    load_order.start()
    pl.semaphore_wait(barrier, len(peers))

    def gather_copy(par, q, i):
        block = gathered.at[par, q, mine]
        return remote(
            block, block, gs_sem.at[q], gr_sem.at[par, q, GATHER_ORDER[i][0]], unit_peers[i]
        )

    def hand_copy(par, q, i):
        block = gathered.at[par, q, pl.ds(hand_slots[i], 2)]
        return remote(block, block, fs_sem.at[q], fr_sem.at[par, q, i], partner)

    def x_copy(par, q, d, p):
        blocks = pl.ds(*PARTS[p])
        return remote(
            outgoing.at[q, x_slots[d], blocks],
            from_x.at[par, q, d - 1, blocks],
            xs_sem.at[q],
            xr_sem.at[par, q, p],
            x_peers[d],
        )

    def z_copy(par, q, d):
        return remote(
            partial.at[q, DISTANCES.index(d)],
            from_z.at[par, q, d - 1],
            zs_sem.at[q],
            zr_sem.at[par, q],
            z_peers[d],
        )

    def split(i):
        step, q = i // CHUNKS, lax.rem(i, CHUNKS)
        return step, q, lax.rem(step, 2)

    def send_gather(par, q):
        for i in reversed(range(len(GATHER_ORDER))):
            gather_copy(par, q, i).start()

    def fill_field(par, q, c, d):
        for n in range(2):
            u = y_units[d] + n
            for h in range(halves):
                value = gathered[par, q, c * 8 + u, :, h * tile : (h + 1) * tile]
                high = value.astype(jnp.bfloat16).astype(jnp.float32)
                both = jnp.concatenate([high, value - high], axis=0)
                field[(u * 2 + c) * halves + h] = both.astype(jnp.bfloat16)

    def hand_over(i):
        _, q, par = split(i)
        for d in (0, 1, 3, 2):
            blocks = pl.ds(hand_slots[0], 1 if d == 0 else 2)
            wait_bytes(gathered.at[par, q, blocks], gr_sem.at[par, q, d])
            hand_copy(par, q, d).start()
            fill_field(par, q, core, d)
        wait_bytes(gathered.at[par, q, pl.ds(core * 8, 7)], gs_sem.at[q])

    def multiply(i):
        _, q, par = split(i)
        wait_bytes(gathered.at[par, q, pl.ds(core * 8, 8)], fs_sem.at[q])
        for d in (0, 1, 3, 2):
            wait_bytes(gathered.at[par, q, pl.ds(8 - core * 8, 2)], fr_sem.at[par, q, d])
            fill_field(par, q, 1 - core, d)
        carried = jnp.zeros((size, tile), jnp.float32)
        for s in range(slots):
            slot = order[0, s]
            both = field[order[1, s]]
            by_high = jnp.dot(both, tiles_hi[slot], preferred_element_type=jnp.float32)
            if size % 16 == 0:
                both = both[:size]
            by_low = jnp.dot(both, tiles_lo[slot], preferred_element_type=jnp.float32)
            product = by_high[:size] + by_high[size:] + by_low[:size]
            if size % 16:
                product = product + by_low[size:]
            carried = product + order[2, s].astype(jnp.float32) * carried
            running[s] = carried
        for n in range(row_tiles):
            block, h = n // halves, n % halves
            outgoing[q, block % 4, z_slots[block // 4], :, h * tile : (h + 1) * tile] = running[order[3, n]]
        for p in range(len(PARTS)):
            for d in (2, 1, 3):
                x_copy(par, q, d, p).start()

    def reduce_x(i, p):
        _, q, par = split(i)
        start, count = PARTS[p]
        wait_bytes(from_x.at[par, q, :, pl.ds(start, count)], xr_sem.at[par, q, p])
        for b in range(start, start + count):
            partial[q, b] = (
                outgoing[q, x, b] + from_x[par, q, 0, b] + from_x[par, q, 2, b]
            ) + from_x[par, q, 1, b]
        for d in (2, 1, 3):
            if d in DISTANCES[start : start + count]:
                z_copy(par, q, d).start()

    def reduce_z(i):
        step, q, par = split(i)
        reduce_x(i, len(PARTS) - 1)
        wait_bytes(from_z.at[par, q], zr_sem.at[par, q])
        wait_bytes(partial.at[q, pl.ds(0, 3)], zs_sem.at[q])
        wait_bytes(outgoing.at[q, pl.ds(0, 3)], xs_sem.at[q])
        value = 0.9 * ((partial[q, 3] + from_z[par, q, 0] + from_z[par, q, 2]) + from_z[par, q, 1])
        rows = pl.ds(pl.multiple_of(q * size, size), size)

        @pl.when(step < STEPS - 1)
        def _():
            gathered[1 - par, q, mine] = value
            send_gather(1 - par, q)
            tele[rows] = tele[rows] + 0.1 * value

        @pl.when(step == STEPS - 1)
        def _():
            grad_out[rows] = value

    def head_copies(stage):
        if stage == 0:
            return [
                remote(head_x.at[x], head_x.at[x], hs_sem.at[d - 1], hr_sem.at[d - 1], at_x(d))
                for d in (2, 1, 3)
            ]
        if stage == 1:
            return [
                remote(
                    head_z.at[z_hi], head_z.at[z_hi], hs_sem.at[d + 2], hr_sem.at[d + 2], at_z(d)
                )
                for d in (2, 1, 3)
            ]
        if stage == 2:
            return [
                remote(
                    head_u.at[unit],
                    head_u.at[unit],
                    hs_sem.at[6 + i],
                    hr_sem.at[6 + i],
                    at_unit(*GATHER_ORDER[i]),
                )
                for i in range(len(GATHER_ORDER))
            ]
        return [remote(head_c.at[core], head_c.at[core], hs_sem.at[13], hr_sem.at[13], partner)]

    def head_stage(stage):
        if stage == 0:
            value = lax.dot_general(
                features[...],
                tele[...],
                (((1,), (1,)), ((), ())),
                precision=lax.Precision.HIGHEST,
                preferred_element_type=jnp.float32,
            )
        else:
            for copy in head_copies(stage - 1):
                copy.wait()
            source = (head_x, head_z, head_u, head_c)[stage - 1]
            value = source[0]
            for n in range(1, source.shape[0]):
                value = value + source[n]
        if stage == 0:
            head_x[x] = value
        elif stage == 1:
            head_z[z_hi] = value
        elif stage == 2:
            head_u[unit] = value
        elif stage == 3:
            head_c[core] = value
        else:
            head_out[...] = value
        if stage < 4:
            for copy in head_copies(stage):
                copy.start()

    send_gather(0, 0)

    def convert_piece(i, carry):
        load_piece(i).wait()
        for n in range(per_piece):
            value = staged[i * per_piece + n]
            high = value.astype(jnp.bfloat16)
            tiles_hi[i * per_piece + n] = high
            tiles_lo[i * per_piece + n] = (value - high.astype(jnp.float32)).astype(jnp.bfloat16)
        return carry

    lax.fori_loop(0, PIECES, convert_piece, 0)
    load_order.wait()
    load_features.wait()
    running[slots] = jnp.zeros((size, tile), jnp.float32)
    hand_over(0)
    for q in range(1, CHUNKS):
        send_gather(0, q)

    head_from = (STEPS - 1) * CHUNKS - 1 + LAG_Z

    def turn(j, carry):
        @pl.when(j < total)
        def _():
            multiply(j)

        @pl.when((j >= LAG_X) & (j < total + LAG_X))
        def _():
            reduce_x(j - LAG_X, 0)
            reduce_x(j - LAG_X, 1)

        @pl.when(j >= LAG_Z)
        def _():
            reduce_z(j - LAG_Z)

        @pl.when(j + 1 < total)
        def _():
            hand_over(j + 1)

        for stage in range(5):

            @pl.when(j == head_from + stage)
            def _():
                head_stage(stage)

        return carry

    lax.fori_loop(0, total + LAG_Z, turn, 0)


def hand_out(*refs):
    for source, target in zip(refs[:3], refs[3:]):
        target[...] = source[...]


def slot_order(tile_rows, tile_cols, live, row_count):
    slots = tile_rows.shape[1]

    def index(shape, dim):
        return lax.broadcasted_iota(jnp.int32, shape, dim)

    def total(values, dim):
        return jnp.sum(values, axis=dim, keepdims=True)

    def upright(values):
        square = (slots, slots)
        return total(jnp.where(index(square, 0) == index(square, 1), values, 0), 1)

    across = index((1, slots), 1)
    down = index((slots, 1), 0)
    key = jnp.where(across < live, tile_rows, row_count) * slots + across
    key_down = upright(key)
    rank = total(jnp.where(key < key_down, 1, 0), 1)
    chosen = rank == across
    slot = total(jnp.where(chosen, down, 0), 0)
    column = total(jnp.where(chosen, upright(tile_cols), 0), 0)
    place = index((1, 128), 1)
    starts = place * slots
    upto = total(jnp.where(key_down < starts + slots, 1, 0), 0)
    below = total(jnp.where(key_down < starts, 1, 0), 0)
    last = jnp.where(upto > below, upto - 1, slots)
    first = total(jnp.where(chosen, total(jnp.where(key < key_down - upright(across), 1, 0), 1), 0), 0)
    keep = jnp.where(first < across, 1, 0)
    return slot, column, keep, last


def shards(final_logits, labels, features, tiles, tile_rows, tile_cols, live):
    classes, width = final_logits.shape
    units = features.shape[0]
    slots, tile = tiles.shape[2], tiles.shape[3]
    size = classes // CHUNKS
    row_count = 16 * width // tile
    f32 = jnp.float32
    vmem = pl.BlockSpec(memory_space=pltpu.VMEM)
    far = pl.BlockSpec(memory_space=pl.ANY)
    dma = pltpu.SemaphoreType.DMA
    parts = pl.pallas_call(
        kernel,
        out_shape=(
            jax.ShapeDtypeStruct((classes, width), f32),
            jax.ShapeDtypeStruct((classes, width), f32),
            jax.ShapeDtypeStruct((units, classes), f32),
        ),
        in_specs=[
            pl.BlockSpec(memory_space=pltpu.SMEM),
            vmem,
            vmem,
            vmem,
            far,
            far,
            far,
        ],
        out_specs=(vmem, vmem, vmem),
        scratch_shapes=[
            pltpu.VMEM((classes, width), f32),
            pltpu.VMEM((units, width), f32),
            pltpu.VMEM((4, 128), jnp.int32),
            pltpu.SMEM((4, 128), jnp.int32),
            pltpu.VMEM((slots, tile, tile), f32),
            pltpu.VMEM((slots, tile, tile), jnp.bfloat16),
            pltpu.VMEM((slots, tile, tile), jnp.bfloat16),
            pltpu.VMEM((row_count, 2 * size, tile), jnp.bfloat16),
            pltpu.VMEM((slots + 1, size, tile), f32),
            pltpu.VMEM((2, CHUNKS, 16, size, width), f32),
            pltpu.VMEM((CHUNKS, 4, 4, size, width), f32),
            pltpu.VMEM((2, CHUNKS, 3, 4, size, width), f32),
            pltpu.VMEM((CHUNKS, 4, size, width), f32),
            pltpu.VMEM((2, CHUNKS, 3, size, width), f32),
            pltpu.VMEM((4, units, classes), f32),
            pltpu.VMEM((4, units, classes), f32),
            pltpu.VMEM((8, units, classes), f32),
            pltpu.VMEM((2, units, classes), f32),
            dma((PIECES,)),
            dma((CHUNKS,)),
            dma((2, CHUNKS, 4)),
            dma((CHUNKS,)),
            dma((2, CHUNKS, 4)),
            dma((CHUNKS,)),
            dma((2, CHUNKS, len(PARTS))),
            dma((CHUNKS,)),
            dma((2, CHUNKS)),
            dma((14,)),
            dma((14,)),
            dma((3,)),
        ],
        compiler_params=pltpu.CompilerParams(
            collective_id=0, has_side_effects=True, vmem_limit_bytes=56 * 2**20
        ),
        cost_estimate=pl.CostEstimate(
            flops=3 * 2 * STEPS * slots * classes * tile * tile,
            bytes_accessed=slots * tile * tile * 4,
            transcendentals=classes * width,
        ),
    )(
        live,
        tile_rows[0],
        tile_cols[0],
        labels.reshape(1, width),
        final_logits,
        features,
        tiles,
    )
    return pl.pallas_call(
        hand_out,
        out_shape=tuple(jax.ShapeDtypeStruct(part.shape, f32) for part in parts),
        in_specs=[vmem] * 3,
        out_specs=(vmem,) * 3,
    )(*parts)


def solution(mesh):
    in_specs = (
        P(None, ("row", "col")),
        P(("row", "col")),
        P(None, ("row", "col")),
        P("row", "col", None, None, None),
        P("row", "col", None),
        P("row", "col", None),
        P("row", "col"),
    )
    out_specs = (P(None, ("row", "col")), P(None, ("row", "col")), P())
    return jax.shard_map(shards, mesh=mesh, in_specs=in_specs, out_specs=out_specs, check_vma=False)
```
